32 devices in a mesh: groups: 2 (over y), rowf: 4 (over z), colf: 4 (over x, core).
Axes of the slice: x: 2, y: 2, z: 4, core: 2. Of those that a mesh axis runs over, the one named last changes fastest.
Arguments:
- embeddings: bfloat16 [1024, 256, 64], P(('groups', 'rowf'), 'colf'), parts along dimension 0, may hold values from -6 to 6
- pair_weights: bfloat16 [256, 128, 64, 64], P('colf', 'rowf'), may hold values from -0.09375 to 0.09375
- upstream: bfloat16 [1024, 256, 128], P('groups', 'colf', 'rowf'), parts along dimension 0, may hold values from -1.5 to 1.5
Outputs:
- interact: bfloat16 [1024, 256, 128], P('groups', 'colf', 'rowf'), parts along dimension 0
- grad_pair: bfloat16 [512, 128, 64, 64], P(('groups', 'colf'), 'rowf'), parts along dimension 0
- grad_emb: float32 [1024, 256, 64], P(('groups', 'rowf'), 'colf'), parts along dimension 0
The draws below stay inside these ranges and needn't reach their ends.
There are 2 independent parts, one for each index of `groups`. The reference program is written for one: setup_inputs(seed, part) draws one part's arguments, and reference() takes and returns one part's arrays. A program takes and returns all parts, laid end to end along the dimension named above; an argument that names none is the same for every part. Nothing has to cross between parts.
All inputs are finite; a program needn't handle non-finite values.
Results may differ from the reference program's by a relative error of at most 0.0049.
Values may be sent and summed in bfloat16 or wider, within the bound.
A program may use at most 320 MiB of HBM per device.

```python
import jax
import jax.numpy as jnp
from jax import lax

FIELDS = 256
EMB = 64
BATCH = 512
HALF = 128


def block_levels(rng, dims, pieces, least, largest):
    def one(axis_at, parts):
        steps = jax.random.uniform(jax.random.fold_in(jax.random.fold_in(rng, 6), axis_at), (parts,), jnp.float32, least / len(pieces), largest / len(pieces))
        return jnp.repeat(jnp.exp(steps), dims[axis_at] // parts).reshape((-1,) + (1,) * (len(dims) - axis_at - 1))

    gain = one(*pieces[0])
    for cut in pieces[1:]:
        gain = gain * one(*cut)
    return gain


def gaussian(key, extent, width, bound, split=(), kind=jnp.bfloat16):
    values = jax.random.normal(key, extent, jnp.float32) * width
    if len(split) > 0:
        values = block_levels(key, extent, split, -0.22, 0.18) * values
    return jnp.clip(values, min=-bound, max=bound).astype(kind)


def setup_inputs(seed: int = 0, part: int = 0) -> dict:
    streams_of = jax.random.split(jax.random.key(seed), 4)
    own_keys = jax.random.split(jax.random.fold_in(streams_of[3], part), 4)
    embeddings = gaussian(own_keys[0], (BATCH, FIELDS, EMB), 1.0, 6.0, ((0, 4), (1, 4)))
    pair_weights = gaussian(streams_of[1], (FIELDS, HALF, EMB, EMB), (EMB * EMB) ** -0.5, 0.09375, ((0, 4), (1, 4)))
    upstream = gaussian(own_keys[2], (BATCH, FIELDS, HALF), 0.25, 1.5, ((1, 4), (2, 4)))
    return {"embeddings": embeddings, "pair_weights": pair_weights, "upstream": upstream}


HIGH = lax.Precision.HIGHEST


def reference(embeddings, pair_weights, upstream):
    emb_float = embeddings.astype(jnp.float32)
    offsets = jnp.arange(HALF, dtype=jnp.int32)
    count_blocks = FIELDS // 8

    def visit(col_total, block_idx):
        row_start = (block_idx * 8).astype(jnp.int32)
        first_ids = row_start + jnp.arange(8, dtype=jnp.int32)
        partner_ids = ((first_ids[:, None] + offsets[None, :] + 1) % FIELDS).astype(jnp.int32)
        dead = jnp.logical_and(offsets[None, :] == HALF - 1, first_ids[:, None] >= HALF)
        pair_mask = 1.0 - dead.astype(jnp.float32)
        weight_rows = lax.dynamic_slice_in_dim(pair_weights, row_start, 8, 0).astype(jnp.float32)
        emb_rows = lax.dynamic_slice_in_dim(emb_float, row_start, 8, 1)
        up_rows = lax.dynamic_slice_in_dim(upstream, row_start, 8, 1).astype(jnp.float32)
        partner = emb_float[:, partner_ids]
        projected = jnp.einsum('bik,ijkl->bijl', emb_rows, weight_rows, precision=HIGH)
        interact = (jnp.sum(projected * partner, axis=3) * pair_mask).astype(jnp.bfloat16)
        scaled = up_rows * pair_mask
        weighted = (scaled[..., None] * partner).astype(jnp.bfloat16)
        weighted = lax.optimization_barrier(weighted).astype(jnp.float32)
        grad_pair = jnp.einsum('bik,bijl->ijkl', emb_rows, weighted, precision=HIGH).astype(jnp.bfloat16)
        row_terms = jnp.einsum('bijl,ijkl->bik', weighted, weight_rows, precision=HIGH)
        col_piece = scaled[..., None] * projected
        col_total = col_total.at[:, partner_ids.reshape(-1)].add(col_piece.reshape(BATCH, 8 * HALF, EMB))
        return col_total, (interact, grad_pair, row_terms)

    start_total = jnp.zeros((BATCH, FIELDS, EMB), jnp.float32)
    col_total, (interact, grad_pair, row_terms) = lax.scan(visit, start_total, jnp.arange(count_blocks, dtype=jnp.int32))
    interact = jnp.transpose(interact, (1, 0, 2, 3)).reshape(BATCH, FIELDS, HALF)
    grad_pair = grad_pair.reshape(FIELDS, HALF, EMB, EMB)
    row_terms = jnp.transpose(row_terms, (1, 0, 2, 3)).reshape(BATCH, FIELDS, EMB)
    grad_emb = row_terms + col_total
    return (interact, grad_pair, grad_emb)
```

```python
import functools

import jax
import jax.numpy as jnp
from jax import lax
from jax.experimental import pallas as pl
from jax.experimental.pallas import tpu as pltpu
from jax.sharding import PartitionSpec as P

F32 = jnp.float32
BF16 = jnp.bfloat16
MEMBERS = 4


def pair_kernel(dead_ref, own_ref, up_ref, weight_ref, near_ref, far_ref, *rest, with_start):
    if with_start:
        start_ref, _, _, *rest = rest
    (interact_ref, grad_ref, row_ref, col_near_ref, col_far_ref, window, col, sems) = rest
    step = pl.program_id(0)
    n_off = weight_ref.shape[1]
    width, batch = own_ref.shape[1:]

    @pl.when(step == 0)
    def _():
        copies = [
            pltpu.make_async_copy(near_ref, window.at[pl.ds(0, n_off)], sems.at[0]),
            pltpu.make_async_copy(far_ref, window.at[pl.ds(n_off, n_off)], sems.at[1]),
        ]
        if with_start:
            copies.append(pltpu.make_async_copy(start_ref, col.at[pl.ds(0, n_off)], sems.at[2]))
        else:
            col[0:n_off] = jnp.zeros((n_off, width, batch), F32)
        for copy in copies:
            copy.start()
        col[n_off:] = jnp.zeros((n_off, width, batch), F32)
        for copy in copies:
            copy.wait()

    own = own_ref[0]
    rows = lax.broadcasted_iota(jnp.int32, (n_off, batch), 0)
    dead = jnp.logical_and(rows == n_off - 1, step >= dead_ref[0])
    scaled = jnp.where(dead, 0.0, up_ref[0].astype(F32))
    total = jnp.zeros((width, batch), F32)
    dots = []
    for first in range(0, n_off, MEMBERS):
        members = range(first, first + MEMBERS)
        mats = [weight_ref[0, d] for d in members]
        weighted = jnp.concatenate(
            [window[step + d + 1] * scaled[d : d + 1].astype(BF16) for d in members], axis=0
        )
        turned = jnp.concatenate([mat.T for mat in mats], axis=0)
        projected = jnp.dot(turned, own, preferred_element_type=F32)
        for at, d in enumerate(members):
            piece = projected[at * width : (at + 1) * width]
            partner = window[step + d + 1].astype(F32)
            dots.append(jnp.sum(piece * partner, axis=0, keepdims=True))
            col[step + d + 1] += scaled[d : d + 1] * piece
        total = total + jnp.dot(
            jnp.concatenate(mats, axis=1), weighted, preferred_element_type=F32
        )
        grads = lax.dot_general(
            weighted, own, (((1,), (1,)), ((), ())), preferred_element_type=F32
        )
        for at, d in enumerate(members):
            grad_ref[0, d] = grads[at * width : (at + 1) * width].T.astype(BF16)
    interact = jnp.where(dead, 0.0, jnp.concatenate(dots, axis=0))
    interact_ref[0] = interact.astype(BF16)
    row_ref[0] = total

    @pl.when(step == pl.num_programs(0) - 1)
    def _():
        col_near_ref[...] = col[0:n_off].astype(col_near_ref.dtype)
        col_far_ref[...] = col[n_off:].astype(col_far_ref.dtype)


def pair_block(part, dead_from, own, up, weights, near, far, earlier, far_type):
    n_off, width = weights.shape[1], weights.shape[2]
    batch = own.shape[2]
    block = (n_off, width, batch)
    anywhere = pl.BlockSpec(memory_space=pl.ANY)
    pairs = n_off * n_off
    in_specs = [
        pl.BlockSpec(memory_space=pltpu.SMEM),
        pl.BlockSpec((1, width, batch), lambda i: (i, 0, 0)),
        pl.BlockSpec((1, n_off, batch), lambda i: (part * n_off + i, 0, 0)),
        pl.BlockSpec((1, n_off, width, width), lambda i: (part * n_off + i, 0, 0, 0)),
        anywhere,
        anywhere,
    ]
    args = [dead_from, own, up, weights, near, far]
    aliases = {}
    if earlier:
        aliases = {len(args) + 1: 0, len(args) + 2: 1}
        in_specs += [anywhere] * 3
        args += earlier
    whole = pl.BlockSpec(block, lambda i: (0, 0, 0), pipeline_mode=pl.Buffered(1))
    return pl.pallas_call(
        functools.partial(pair_kernel, with_start=len(earlier) > 0),
        grid=(n_off,),
        in_specs=in_specs,
        out_specs=[
            pl.BlockSpec((1, n_off, batch), lambda i: (part * n_off + i, 0, 0)),
            pl.BlockSpec((1, n_off, width, width), lambda i: (part * n_off + i, 0, 0, 0)),
            pl.BlockSpec((1, width, batch), lambda i: (i, 0, 0)),
            whole,
            whole,
        ],
        out_shape=[
            jax.ShapeDtypeStruct(up.shape, BF16),
            jax.ShapeDtypeStruct(weights.shape, BF16),
            jax.ShapeDtypeStruct(block, F32),
            jax.ShapeDtypeStruct(block, BF16),
            jax.ShapeDtypeStruct(block, far_type),
        ],
        scratch_shapes=[
            pltpu.VMEM((2 * n_off, width, batch), BF16),
            pltpu.VMEM((2 * n_off, width, batch), F32),
            pltpu.SemaphoreType.DMA((3,)),
        ],
        input_output_aliases=aliases,
        compiler_params=pltpu.CompilerParams(vmem_limit_bytes=52 * 2**20),
        cost_estimate=pl.CostEstimate(
            flops=24 * pairs * batch * width * width,
            bytes_accessed=8 * pairs * width * width,
            transcendentals=0,
        ),
    )(*args)


def choose(options, index):
    out = options[0]
    for at in range(1, len(options)):
        out = jnp.where(index == at, options[at], out)
    return out


def shards(embeddings, pair_weights, upstream):
    n_rowf, n_colf = lax.axis_size("rowf"), lax.axis_size("colf")
    row_id, col_id = lax.axis_index("rowf"), lax.axis_index("colf")
    a_dev, off_dev = pair_weights.shape[0], pair_weights.shape[1]
    half_fields = off_dev * n_rowf
    parts = a_dev // off_dev
    emb = jnp.transpose(embeddings, (1, 2, 0))
    up = jnp.transpose(upstream, (1, 2, 0))

    def moved(block, distance, back=False):
        pairs = []
        for r in range(n_rowf):
            for c in range(n_colf):
                ahead = r * n_colf + (c + distance(r)) % n_colf
                here = r * n_colf + c
                pairs.append((here, ahead) if back else (ahead, here))
        return lax.ppermute(block, ("rowf", "colf"), pairs)

    own = [
        lax.all_gather(emb[m * off_dev : (m + 1) * off_dev], "rowf", axis=2, tiled=True)
        for m in range(parts)
    ]
    fetched = [
        moved(own[m], lambda r, m=m: (r + (m - r) % parts) // parts) for m in range(parts)
    ]
    windows = [choose(fetched, (row_id + w) % parts) for w in range(parts)]
    windows.append(moved(choose(own, row_id % parts), lambda r: (r + parts) // parts))

    row_parts, returned, earlier = [], [], []
    for part in range(parts):
        last = part == parts - 1
        dead_from = half_fields - col_id * a_dev - part * off_dev
        dead_from = jnp.where(row_id == n_rowf - 1, dead_from, off_dev).astype(jnp.int32)
        interact, grad, row, near, far = pair_block(
            part, dead_from.reshape(1), own[part], up, pair_weights,
            windows[part], windows[part + 1], earlier, BF16 if last else F32,
        )
        row_parts.append(row)
        returned.append(moved(near, lambda r, w=part: (r + w) // parts, True))
        earlier = [far, interact, grad]
    returned.append(moved(far, lambda r: (r + parts) // parts, True))
    terms = [item.astype(F32) for item in returned]
    terms = [terms[0] + terms[parts]] + terms[1:parts]
    outs = []
    for m in range(parts):
        carried = choose(terms, (m - row_id) % parts)
        summed = (row_parts[m] + carried).astype(BF16)
        outs.append(lax.psum_scatter(summed, "rowf", scatter_dimension=2, tiled=True))
    grad_emb = jnp.concatenate(outs, axis=0).astype(F32)
    return (
        jnp.transpose(interact, (2, 0, 1)),
        grad,
        jnp.transpose(grad_emb, (2, 0, 1)),
    )


def solution(mesh):
    return jax.shard_map(
        shards,
        mesh=mesh,
        in_specs=(
            P(("groups", "rowf"), "colf", None),
            P("colf", "rowf", None, None),
            P("groups", "colf", "rowf"),
        ),
        out_specs=(
            P("groups", "colf", "rowf"),
            P(("groups", "colf"), "rowf", None, None),
            P(("groups", "rowf"), "colf", None),
        ),
        check_vma=False,
    )
```

```python
import functools

import jax
import jax.numpy as jnp
from jax import lax
from jax.experimental import pallas as pl
from jax.experimental.pallas import tpu as pltpu
from jax.sharding import PartitionSpec as P

F32 = jnp.float32
BF16 = jnp.bfloat16
MEMBERS = 4


def pair_kernel(dead_ref, own_ref, up_ref, weight_ref, near_ref, far_ref, *rest, with_start):
    if with_start:
        start_ref, _, _, *rest = rest
    (interact_ref, grad_ref, row_ref, col_near_ref, col_far_ref, window, col, sems) = rest
    step = pl.program_id(0)
    n_off = weight_ref.shape[1]
    width, batch = own_ref.shape[1:]

    @pl.when(step == 0)
    def _():
        copies = [
            pltpu.make_async_copy(near_ref, window.at[pl.ds(0, n_off)], sems.at[0]),
            pltpu.make_async_copy(far_ref, window.at[pl.ds(n_off, n_off)], sems.at[1]),
        ]
        if with_start:
            copies.append(pltpu.make_async_copy(start_ref, col.at[pl.ds(0, n_off)], sems.at[2]))
        else:
            col[0:n_off] = jnp.zeros((n_off, width, batch), F32)
        for copy in copies:
            copy.start()
        col[n_off:] = jnp.zeros((n_off, width, batch), F32)
        for copy in copies:
            copy.wait()

    own = own_ref[0]
    rows = lax.broadcasted_iota(jnp.int32, (n_off, batch), 0)
    dead = jnp.logical_and(rows == n_off - 1, step >= dead_ref[0])
    scaled = jnp.where(dead, 0.0, up_ref[0].astype(F32))
    total = jnp.zeros((width, batch), F32)
    dots = []
    for first in range(0, n_off, MEMBERS):
        members = range(first, first + MEMBERS)
        mats = [weight_ref[0, d] for d in members]
        weighted = jnp.concatenate(
            [window[step + d + 1] * scaled[d : d + 1].astype(BF16) for d in members], axis=0
        )
        turned = jnp.concatenate([mat.T for mat in mats], axis=0)
        projected = jnp.dot(turned, own, preferred_element_type=F32)
        for at, d in enumerate(members):
            piece = projected[at * width : (at + 1) * width]
            partner = window[step + d + 1].astype(F32)
            dots.append(jnp.sum(piece * partner, axis=0, keepdims=True))
            col[step + d + 1] += scaled[d : d + 1] * piece
        total = total + jnp.dot(
            jnp.concatenate(mats, axis=1), weighted, preferred_element_type=F32
        )
        grads = lax.dot_general(
            weighted, own, (((1,), (1,)), ((), ())), preferred_element_type=F32
        )
        for at, d in enumerate(members):
            grad_ref[0, d] = grads[at * width : (at + 1) * width].T.astype(BF16)
    interact = jnp.where(dead, 0.0, jnp.concatenate(dots, axis=0))
    interact_ref[0] = interact.astype(BF16)
    row_ref[0] = total

    @pl.when(step == pl.num_programs(0) - 1)
    def _():
        col_near_ref[...] = col[0:n_off].astype(col_near_ref.dtype)
        col_far_ref[...] = col[n_off:].astype(col_far_ref.dtype)


def pair_block(part, dead_from, own, up, weights, near, far, earlier, far_type):
    n_off, width = weights.shape[1], weights.shape[2]
    batch = own.shape[2]
    block = (n_off, width, batch)
    anywhere = pl.BlockSpec(memory_space=pl.ANY)
    pairs = n_off * n_off
    in_specs = [
        pl.BlockSpec(memory_space=pltpu.SMEM),
        pl.BlockSpec((1, width, batch), lambda i: (i, 0, 0)),
        pl.BlockSpec((1, n_off, batch), lambda i: (part * n_off + i, 0, 0)),
        pl.BlockSpec((1, n_off, width, width), lambda i: (part * n_off + i, 0, 0, 0)),
        anywhere,
        anywhere,
    ]
    args = [dead_from, own, up, weights, near, far]
    aliases = {}
    if earlier:
        aliases = {len(args) + 1: 0, len(args) + 2: 1}
        in_specs += [anywhere] * 3
        args += earlier
    whole = pl.BlockSpec(block, lambda i: (0, 0, 0), pipeline_mode=pl.Buffered(1))
    return pl.pallas_call(
        functools.partial(pair_kernel, with_start=len(earlier) > 0),
        grid=(n_off,),
        in_specs=in_specs,
        out_specs=[
            pl.BlockSpec((1, n_off, batch), lambda i: (part * n_off + i, 0, 0)),
            pl.BlockSpec((1, n_off, width, width), lambda i: (part * n_off + i, 0, 0, 0)),
            pl.BlockSpec((1, width, batch), lambda i: (i, 0, 0)),
            whole,
            whole,
        ],
        out_shape=[
            jax.ShapeDtypeStruct(up.shape, BF16),
            jax.ShapeDtypeStruct(weights.shape, BF16),
            jax.ShapeDtypeStruct(block, F32),
            jax.ShapeDtypeStruct(block, BF16),
            jax.ShapeDtypeStruct(block, far_type),
        ],
        scratch_shapes=[
            pltpu.VMEM((2 * n_off, width, batch), BF16),
            pltpu.VMEM((2 * n_off, width, batch), F32),
            pltpu.SemaphoreType.DMA((3,)),
        ],
        input_output_aliases=aliases,
        compiler_params=pltpu.CompilerParams(vmem_limit_bytes=52 * 2**20),
        cost_estimate=pl.CostEstimate(
            flops=24 * pairs * batch * width * width,
            bytes_accessed=8 * pairs * width * width,
            transcendentals=0,
        ),
    )(*args)


def choose(options, index):
    out = options[0]
    for at in range(1, len(options)):
        out = jnp.where(index == at, options[at], out)
    return out


def shards(embeddings, pair_weights, upstream):
    n_rowf, n_colf = lax.axis_size("rowf"), lax.axis_size("colf")
    row_id, col_id = lax.axis_index("rowf"), lax.axis_index("colf")
    a_dev, off_dev = pair_weights.shape[0], pair_weights.shape[1]
    half_fields = off_dev * n_rowf
    parts = a_dev // off_dev
    emb = jnp.transpose(embeddings, (1, 2, 0))
    up = jnp.transpose(upstream, (1, 2, 0))

    def moved(block, distance, back=False):
        pairs = []
        for r in range(n_rowf):
            for c in range(n_colf):
                ahead = r * n_colf + (c + distance(r)) % n_colf
                here = r * n_colf + c
                pairs.append((here, ahead) if back else (ahead, here))
        return lax.ppermute(block, ("rowf", "colf"), pairs)

    own = [
        lax.all_gather(emb[m * off_dev : (m + 1) * off_dev], "rowf", axis=2, tiled=True)
        for m in range(parts)
    ]
    fetched = [
        moved(own[m], lambda r, m=m: (r + (m - r) % parts) // parts) for m in range(parts)
    ]
    windows = [choose(fetched, (row_id + w) % parts) for w in range(parts)]
    held = choose(own, row_id % parts)
    held, windows[parts - 1] = lax.optimization_barrier((held, windows[parts - 1]))
    windows.append(moved(held, lambda r: (r + parts) // parts))

    row_parts, cols, earlier = [], [], []
    for part in range(parts):
        last = part == parts - 1
        dead_from = half_fields - col_id * a_dev - part * off_dev
        dead_from = jnp.where(row_id == n_rowf - 1, dead_from, off_dev).astype(jnp.int32)
        interact, grad, row, near, far = pair_block(
            part, dead_from.reshape(1), own[part], up, pair_weights,
            windows[part], windows[part + 1], earlier, BF16 if last else F32,
        )
        row_parts.append(row)
        cols.append(near)
        earlier = [far, interact, grad]
    cols.append(far)
    first_back = moved(cols[0], lambda r: r // parts, True)
    outs = []
    shape = (off_dev, emb.shape[1], n_rowf, emb.shape[2])
    backs = []
    for m in range(parts):
        sent = choose(cols[1:], (m - row_id - 1) % parts)
        if m == 0:
            sent, first_back = lax.optimization_barrier((sent, first_back))
        else:
            sent, backs[-1] = lax.optimization_barrier((sent, backs[-1]))
        backs.append(moved(sent, lambda r, m=m: (r + (m - r - 1) % parts + 1) // parts, True))
    for m in range(parts):
        if m > 0:
            backs[m], summed = lax.optimization_barrier((backs[m], summed))
        summed = row_parts[m] + backs[m].astype(F32)
        summed = summed + jnp.where(row_id % parts == m, first_back.astype(F32), 0.0)
        summed = jnp.transpose(summed.astype(BF16).reshape(shape), (2, 0, 1, 3))
        outs.append(lax.psum_scatter(summed, "rowf", scatter_dimension=0, tiled=False))
    grad_emb = jnp.concatenate(outs, axis=0).astype(F32)
    return (
        jnp.transpose(interact, (2, 0, 1)),
        grad,
        jnp.transpose(grad_emb, (2, 0, 1)),
    )


def solution(mesh):
    return jax.shard_map(
        shards,
        mesh=mesh,
        in_specs=(
            P(("groups", "rowf"), "colf", None),
            P("colf", "rowf", None, None),
            P("groups", "colf", "rowf"),
        ),
        out_specs=(
            P("groups", "colf", "rowf"),
            P(("groups", "colf"), "rowf", None, None),
            P(("groups", "rowf"), "colf", None),
        ),
        check_vma=False,
    )
```

```python
import functools

import jax
import jax.numpy as jnp
from jax import lax
from jax.experimental import pallas as pl
from jax.experimental.pallas import tpu as pltpu
from jax.sharding import PartitionSpec as P

F32 = jnp.float32
BF16 = jnp.bfloat16
MEMBERS = 4


def pair_kernel(dead_ref, own_ref, up_ref, weight_ref, near_ref, far_ref, *rest, with_start):
    if with_start:
        start_ref, _, _, *rest = rest
    (interact_ref, grad_ref, row_ref, col_near_ref, col_far_ref, window, col, sems) = rest
    step = pl.program_id(0)
    n_off = weight_ref.shape[1]
    width, batch = own_ref.shape[1:]

    @pl.when(step == 0)
    def _():
        copies = [
            pltpu.make_async_copy(near_ref, window.at[pl.ds(0, n_off)], sems.at[0]),
            pltpu.make_async_copy(far_ref, window.at[pl.ds(n_off, n_off)], sems.at[1]),
        ]
        if with_start:
            copies.append(pltpu.make_async_copy(start_ref, col.at[pl.ds(n_off, n_off)], sems.at[2]))
        else:
            col[n_off:] = jnp.zeros((n_off, width, batch), F32)
        for copy in copies:
            copy.start()
        col[0:n_off] = jnp.zeros((n_off, width, batch), F32)
        for copy in copies:
            copy.wait()

    own = own_ref[0]
    rows = lax.broadcasted_iota(jnp.int32, (n_off, batch), 0)
    dead = jnp.logical_and(rows == n_off - 1, step >= dead_ref[0])
    scaled = jnp.where(dead, 0.0, up_ref[0].astype(F32))
    total = jnp.zeros((width, batch), F32)
    dots = []
    for first in range(0, n_off, MEMBERS):
        members = range(first, first + MEMBERS)
        mats = [weight_ref[0, d] for d in members]
        weighted = jnp.concatenate(
            [window[step + d + 1] * scaled[d : d + 1].astype(BF16) for d in members], axis=0
        )
        turned = jnp.concatenate([mat.T for mat in mats], axis=0)
        projected = jnp.dot(turned, own, preferred_element_type=F32)
        for at, d in enumerate(members):
            piece = projected[at * width : (at + 1) * width]
            partner = window[step + d + 1].astype(F32)
            dots.append(jnp.sum(piece * partner, axis=0, keepdims=True))
            col[step + d + 1] += scaled[d : d + 1] * piece
        total = total + jnp.dot(
            jnp.concatenate(mats, axis=1), weighted, preferred_element_type=F32
        )
        grads = lax.dot_general(
            weighted, own, (((1,), (1,)), ((), ())), preferred_element_type=F32
        )
        for at, d in enumerate(members):
            grad_ref[0, d] = grads[at * width : (at + 1) * width].T.astype(BF16)
    interact = jnp.where(dead, 0.0, jnp.concatenate(dots, axis=0))
    interact_ref[0] = interact.astype(BF16)
    row_ref[0] = total

    @pl.when(step == pl.num_programs(0) - 1)
    def _():
        col_near_ref[...] = col[0:n_off].astype(col_near_ref.dtype)
        col_far_ref[...] = col[n_off:].astype(col_far_ref.dtype)


def pair_block(part, dead_from, own, up, weights, near, far, earlier, near_type):
    n_off, width = weights.shape[1], weights.shape[2]
    batch = own.shape[2]
    block = (n_off, width, batch)
    anywhere = pl.BlockSpec(memory_space=pl.ANY)
    pairs = n_off * n_off
    in_specs = [
        pl.BlockSpec(memory_space=pltpu.SMEM),
        pl.BlockSpec((1, width, batch), lambda i: (i, 0, 0)),
        pl.BlockSpec((1, n_off, batch), lambda i: (part * n_off + i, 0, 0)),
        pl.BlockSpec((1, n_off, width, width), lambda i: (part * n_off + i, 0, 0, 0)),
        anywhere,
        anywhere,
    ]
    args = [dead_from, own, up, weights, near, far]
    aliases = {}
    if earlier:
        aliases = {len(args) + 1: 0, len(args) + 2: 1}
        in_specs += [anywhere] * 3
        args += earlier
    whole = pl.BlockSpec(block, lambda i: (0, 0, 0), pipeline_mode=pl.Buffered(1))
    return pl.pallas_call(
        functools.partial(pair_kernel, with_start=len(earlier) > 0),
        grid=(n_off,),
        in_specs=in_specs,
        out_specs=[
            pl.BlockSpec((1, n_off, batch), lambda i: (part * n_off + i, 0, 0)),
            pl.BlockSpec((1, n_off, width, width), lambda i: (part * n_off + i, 0, 0, 0)),
            pl.BlockSpec((1, width, batch), lambda i: (i, 0, 0)),
            whole,
            whole,
        ],
        out_shape=[
            jax.ShapeDtypeStruct(up.shape, BF16),
            jax.ShapeDtypeStruct(weights.shape, BF16),
            jax.ShapeDtypeStruct(block, F32),
            jax.ShapeDtypeStruct(block, near_type),
            jax.ShapeDtypeStruct(block, BF16),
        ],
        scratch_shapes=[
            pltpu.VMEM((2 * n_off, width, batch), BF16),
            pltpu.VMEM((2 * n_off, width, batch), F32),
            pltpu.SemaphoreType.DMA((3,)),
        ],
        input_output_aliases=aliases,
        compiler_params=pltpu.CompilerParams(vmem_limit_bytes=52 * 2**20),
        cost_estimate=pl.CostEstimate(
            flops=24 * pairs * batch * width * width,
            bytes_accessed=8 * pairs * width * width,
            transcendentals=0,
        ),
    )(*args)


def choose(options, index):
    out = options[0]
    for at in range(1, len(options)):
        out = jnp.where(index == at, options[at], out)
    return out


def shards(embeddings, pair_weights, upstream):
    n_rowf, n_colf = lax.axis_size("rowf"), lax.axis_size("colf")
    row_id, col_id = lax.axis_index("rowf"), lax.axis_index("colf")
    a_dev, off_dev = pair_weights.shape[0], pair_weights.shape[1]
    half_fields = off_dev * n_rowf
    parts = a_dev // off_dev
    emb = jnp.transpose(embeddings, (1, 2, 0))
    up = jnp.transpose(upstream, (1, 2, 0))

    def moved(block, distance, back=False):
        pairs = []
        for r in range(n_rowf):
            for c in range(n_colf):
                ahead = r * n_colf + (c + distance(r)) % n_colf
                here = r * n_colf + c
                pairs.append((here, ahead) if back else (ahead, here))
        return lax.ppermute(block, ("rowf", "colf"), pairs)

    own = [
        lax.all_gather(emb[m * off_dev : (m + 1) * off_dev], "rowf", axis=2, tiled=True)
        for m in range(parts)
    ]
    fetched = [
        moved(own[m], lambda r, m=m: (r + (m - r - 1) % parts + 1) // parts)
        for m in range(parts)
    ]
    windows = [choose(fetched, (row_id + w) % parts) for w in range(1, parts + 1)]
    held = choose(own, row_id % parts)
    if parts > 1:
        held, windows[-1] = lax.optimization_barrier((held, windows[-1]))
    windows = [moved(held, lambda r: r // parts)] + windows

    row_parts, cols, earlier = [None] * parts, [None] * (parts + 1), []
    for part in reversed(range(parts)):
        dead_from = half_fields - col_id * a_dev - part * off_dev
        dead_from = jnp.where(row_id == n_rowf - 1, dead_from, off_dev).astype(jnp.int32)
        interact, grad, row_parts[part], near, cols[part + 1] = pair_block(
            part, dead_from.reshape(1), own[part], up, pair_weights,
            windows[part], windows[part + 1], earlier, BF16 if part == 0 else F32,
        )
        earlier = [near, interact, grad]
    cols[0] = near
    before = first_back = moved(cols[parts], lambda r: (r + parts) // parts, True)
    shape = (off_dev, emb.shape[1], n_rowf, emb.shape[2])
    order = list(reversed(range(parts)))
    backs = [None] * parts
    for m in order:
        sent = choose(cols[:parts], (m - row_id) % parts)
        sent, before = lax.optimization_barrier((sent, before))
        if m == order[0]:
            first_back = before
        else:
            backs[m + 1] = before
        before = moved(sent, lambda r, m=m: (r + (m - r) % parts) // parts, True)
        backs[m] = before
    outs = [None] * parts
    summed = None
    for m in order:
        if summed is not None:
            backs[m], summed = lax.optimization_barrier((backs[m], summed))
        summed = row_parts[m] + backs[m].astype(F32)
        summed = summed + jnp.where(row_id % parts == m, first_back.astype(F32), 0.0)
        summed = jnp.transpose(summed.astype(BF16).reshape(shape), (2, 0, 1, 3))
        outs[m] = lax.psum_scatter(summed, "rowf", scatter_dimension=0, tiled=False)
    grad_emb = jnp.concatenate(outs, axis=0).astype(F32)
    return (
        jnp.transpose(interact, (2, 0, 1)),
        grad,
        jnp.transpose(grad_emb, (2, 0, 1)),
    )


def solution(mesh):
    return jax.shard_map(
        shards,
        mesh=mesh,
        in_specs=(
            P(("groups", "rowf"), "colf", None),
            P("colf", "rowf", None, None),
            P("groups", "colf", "rowf"),
        ),
        out_specs=(
            P("groups", "colf", "rowf"),
            P(("groups", "colf"), "rowf", None, None),
            P(("groups", "rowf"), "colf", None),
        ),
        check_vma=False,
    )
```
